256 devices in a mesh: section: 16 (over x, y), tp: 16 (over z, core).
Axes of the slice: x: 4, y: 4, z: 8, core: 2. Of those that a mesh axis runs over, the one named last changes fastest.
Arguments:
- partials: bfloat16 [16, 16, 128, 16384], P('section', 'tp'), may hold values from -6 to 6, as said below
- residual: bfloat16 [16, 128, 16384], P('section'), may hold values from -54 to 54
Outputs:
- mlp_input: bfloat16 [16, 128, 16384], P('section')
- next_hidden: bfloat16 [16, 128, 16384], P('section', 'tp')
The draws below stay inside these ranges and needn't reach their ends.
Inputs may be any that keep to these rules, and one draw needn't show every extreme that they name: `partials`: every entry is a multiple of 1/64.
All inputs are finite; a program needn't handle non-finite values.
Results may differ from the reference program's by a relative error of at most 0.005.
Values may be sent and summed in bfloat16 or wider, within the bound.
No kernel may reach another device: no remote copies, remote signals or barrier semaphores. Data moves between devices by JAX's collectives and lax.ppermute only.
A program may use at most 128 MiB of HBM per device.

```python
import math
import jax
import jax.numpy as jnp
from jax import lax

D = 16384
BLOCK = 128
ROWS = 128
NBLK = 128
N_SECTION = 16
N_TP = 16


def draw_partials(key, part):
    key = jax.random.fold_in(key, 5)
    key_vals, key_pair = jax.random.split(key)
    reach = 48
    section_keys = jax.random.split(key_vals, N_SECTION)
    pair_keys = jax.random.split(key_pair, N_SECTION)
    pairing = jax.vmap(lambda one_key: jax.random.permutation(one_key, N_TP))(pair_keys)
    row_block = jnp.arange(ROWS, dtype=jnp.int32) // (ROWS // N_TP)

    def one_section(inputs):
        section_key, section_pair = inputs
        counts = jax.random.randint(section_key, (N_TP, ROWS, D), -reach, reach + 1)
        boost = jnp.where(row_block[None, :] == section_pair[:, None], 4, 1)
        return ((counts * boost[:, :, None]).astype(jnp.float32) * 2.0 ** (-6)).astype(jnp.bfloat16)
    return lax.map(one_section, (section_keys, pairing))


def draw_residual(key, part):
    key = jax.random.fold_in(key, 11)
    key_base, key_rows, key_cols = jax.random.split(key, 3)
    values = jnp.clip(jax.random.normal(key_base, (N_SECTION, ROWS, D), jnp.float32), -6.0, 6.0)
    low_end = 0.3
    high_end = 3.0
    row_scale = jnp.exp(jax.random.uniform(key_rows, (N_SECTION, ROWS, 1), jnp.float32, math.log(low_end), math.log(high_end)))
    col_scale = jnp.exp(jax.random.uniform(key_cols, (1, 1, D), jnp.float32, math.log(low_end), math.log(high_end)))
    return (values * row_scale * col_scale).astype(jnp.bfloat16)


def setup_inputs(seed: int = 0) -> dict:
    streams_of = jax.random.split(jax.random.key(seed), 3)
    return {
        "partials": draw_partials(jax.random.fold_in(streams_of[2], 71), 0),
        "residual": draw_residual(jax.random.fold_in(streams_of[2], 71), 0),
    }


coded_peak = 448.0

def hadamard(order):
    index = jnp.arange(order, dtype=jnp.int32)
    common = jnp.bitwise_and(index[:, None], index[None, :])
    parity = jnp.zeros((order, order), jnp.int32)
    for bit_pos in range(int(math.log2(order))):
        parity = parity + jnp.bitwise_and(jnp.right_shift(common, bit_pos), 1)
    return (1 - 2 * jnp.bitwise_and(parity, 1)).astype(jnp.bfloat16)

def block_scale(peak_abs):
    scale = jnp.zeros_like(peak_abs) + 2.0 ** (-16)
    inverse = jnp.zeros_like(peak_abs) + 2.0 ** 16
    for exponent in range(-16, 8):
        above = peak_abs > coded_peak * 2.0 ** exponent
        scale = jnp.where(above, 2.0 ** (exponent + 1), scale)
        inverse = jnp.where(above, 2.0 ** (-exponent - 1), inverse)
    return (scale, inverse)

def coarse_levels(values):
    magnitude = jnp.abs(values)
    quantum = jnp.zeros_like(magnitude) + 2.0 ** (-9)
    inverse = jnp.zeros_like(magnitude) + 2.0 ** 9
    for exponent in range(-5, 9):
        above = magnitude >= 2.0 ** exponent
        quantum = jnp.where(above, 2.0 ** (exponent - 3), quantum)
        inverse = jnp.where(above, 2.0 ** (3 - exponent), inverse)
    levels = jnp.floor(magnitude * inverse + 0.5) * quantum
    return jnp.where(values < 0, -levels, levels)

def reference(partials, residual):
    hadamard_block = hadamard(BLOCK)

    def one_section(inputs):
        shares, stream = inputs
        rotated = jnp.dot(shares.reshape(-1, BLOCK), hadamard_block, preferred_element_type=jnp.float32)
        rotated = rotated.reshape(N_TP, ROWS, NBLK, BLOCK)
        scale, inverse = block_scale(lax.optimization_barrier(jnp.max(jnp.abs(rotated), axis=3)))
        scales = scale.astype(jnp.bfloat16)
        coded = coarse_levels(rotated * inverse[..., None]).astype(jnp.bfloat16)
        values = coded.astype(jnp.float32) * scales.astype(jnp.float32)[..., None]
        summed = lax.optimization_barrier(jnp.sum(values, axis=0)).reshape(ROWS, D) * BLOCK ** (-0.5)
        hidden = (stream.astype(jnp.float32) + summed).astype(jnp.bfloat16)
        hidden_f = hidden.astype(jnp.float32)
        inv_rms = lax.rsqrt(lax.optimization_barrier(jnp.sum(hidden_f * hidden_f, axis=1, keepdims=True)) / D + 1e-05)
        normed = (hidden_f * inv_rms).astype(jnp.bfloat16)
        return (hidden, normed)
    hidden_all, mlp_input = lax.map(one_section, (partials, residual))
    next_hidden = jnp.roll(hidden_all, 1, axis=0)
    return (mlp_input, next_hidden)
```

```python
import jax
import jax.numpy as jnp
import numpy as np
from jax import lax
from jax.experimental import pallas as pl
from jax.experimental.pallas import tpu as pltpu
from jax.sharding import PartitionSpec as P

BLOCK = 128
D = 16384
HALF = D // 2
CHIPS = 8
OWN = 8
STEP_COLS = 4096
UNIT = 2048


def hadamard(order):
    index = np.arange(order)
    common = index[:, None] & index[None, :]
    parity = np.zeros((order, order), np.int64)
    for bit in range(order.bit_length() - 1):
        parity ^= (common >> bit) & 1
    return (1 - 2 * parity).astype(np.float32)


def block_scale(peak):
    units = peak * 1024.0
    below = jnp.floor((units - 1.0) * (1.0 / 7.0) + 1.0 / 64.0).astype(jnp.int32)
    below = jnp.maximum(below, 0)
    for shift in (1, 2, 4, 8, 16):
        below = below | (below >> shift)
    return (below + 1).astype(jnp.float32) * 2.0 ** (-16)


def code(rotated):
    peak = jnp.max(jnp.abs(rotated), axis=1, keepdims=True)
    scale = block_scale(peak)
    nudged = rotated * (1.0 + 2.0 ** (-20))
    wide = nudged * (2.0**20 + 1.0)
    four_bits = wide - (wide - nudged)
    anchor = scale * (1.5 * 2.0**14)
    fixed = (nudged + anchor) - anchor
    return jnp.where(jnp.abs(rotated) < scale * 2.0 ** (-5), fixed, four_bits)


def code_kernel(where_ref, x_ref, h_ref, own_ref, send_ref):
    first = where_ref[1] == 0
    h = h_ref[...]
    for start in range(0, STEP_COLS, UNIT):
        cols = [slice(start + b, start + b + BLOCK) for b in range(0, UNIT, BLOCK)]
        x = jnp.concatenate([x_ref[:, c] for c in cols], axis=0)
        rotated = jnp.dot(x, h, preferred_element_type=jnp.float32)
        values = code(rotated)
        for b, c in enumerate(cols):
            top = values[2 * OWN * b : 2 * OWN * b + OWN]
            low = values[2 * OWN * b + OWN : 2 * OWN * (b + 1)]
            own_ref[:, c] = jnp.where(first, top, low).astype(jnp.bfloat16)
            send_ref[:, c] = jnp.where(first, low, top).astype(jnp.bfloat16)


def code_rows(partials, h, chip, core):
    rows = jax.ShapeDtypeStruct((OWN, D), jnp.bfloat16)
    out = pl.BlockSpec((OWN, STEP_COLS), lambda i, w: (0, i))
    return pl.pallas_call(
        code_kernel,
        out_shape=(rows, rows),
        grid_spec=pltpu.PrefetchScalarGridSpec(
            num_scalar_prefetch=1,
            grid=(D // STEP_COLS,),
            in_specs=[
                pl.BlockSpec((2 * OWN, STEP_COLS), lambda i, w: (w[0], i)),
                pl.BlockSpec((BLOCK, BLOCK), lambda i, w: (0, 0)),
            ],
            out_specs=(out, out),
        ),
        cost_estimate=pl.CostEstimate(
            flops=2 * 2 * OWN * D * BLOCK, bytes_accessed=2 * 2 * 2 * OWN * D, transcendentals=0
        ),
    )(jnp.stack([chip, core]).astype(jnp.int32), partials, h)


def shards(partials, residual):
    h = jnp.asarray(hadamard(BLOCK), jnp.bfloat16)
    local = partials[0, 0]
    place = lax.axis_index("tp")
    chip, core = place // 2, place % 2
    n = 2 * CHIPS

    def ahead(block):
        return lax.ppermute(block, "tp", [(i, (i + 2) % n) for i in range(n)])

    def behind(block):
        return lax.ppermute(block, "tp", [(i, (i - 2) % n) for i in range(n)])

    def other_core(block):
        return lax.ppermute(block, "tp", [(i, i ^ 1) for i in range(n)])

    def chip_sum(k):
        own, send = code_rows(local, h, (chip + k) % CHIPS, core)
        got = other_core(send)
        total = own.astype(jnp.float32) + got.astype(jnp.float32)
        return [total[:, :HALF], total[:, HALF:]]

    up = [None, None]
    down = [None, None]

    def add(total, arrived):
        return total if arrived is None else total + arrived.astype(jnp.float32)

    far = chip_sum(CHIPS // 2)
    up[0] = ahead(far[0].astype(jnp.bfloat16))
    down[1] = behind(far[1].astype(jnp.bfloat16))
    for k in range(CHIPS // 2 - 1, 0, -1):
        up_own, down_own = chip_sum(k), chip_sum(-k)
        for part in (0, 1):
            up[part] = ahead(add(up_own[part], up[part]).astype(jnp.bfloat16))
            down[part] = behind(add(down_own[part], down[part]).astype(jnp.bfloat16))
    near = chip_sum(0)
    rows = lax.dynamic_slice_in_dim(residual[0], place * OWN, OWN, 0).astype(jnp.float32)
    hidden = []
    for part in (0, 1):
        total = add(add(near[part], up[part]), down[part]) * BLOCK ** (-0.5)
        own = rows[:, part * HALF : (part + 1) * HALF]
        hidden.append((own + total).astype(jnp.bfloat16))
    hidden_f = [v.astype(jnp.float32) for v in hidden]
    squares = sum(jnp.sum(v * v, axis=1, keepdims=True) for v in hidden_f)
    inv_rms = lax.rsqrt(squares / D + 1e-05)
    normed = [(v * inv_rms).astype(jnp.bfloat16) for v in hidden_f]

    sections = lax.axis_size("section")
    incoming = lax.ppermute(
        jnp.concatenate(hidden, axis=1), "section", [(i, (i + 1) % sections) for i in range(sections)]
    )

    out = jnp.zeros((2 * OWN * CHIPS, D), jnp.bfloat16)

    def put(out, block, from_chip, part):
        base = (from_chip % CHIPS) * 2 * OWN
        out = lax.dynamic_update_slice(out, block, (base + core * OWN, part * HALF))
        return lax.dynamic_update_slice(
            out, other_core(block), (base + (1 - core) * OWN, part * HALF)
        )

    up, down = list(normed), list(normed)
    for part in (0, 1):
        out = put(out, normed[part], chip, part)
    for k in range(1, CHIPS // 2 + 1):
        for part in (0, 1):
            if k < CHIPS // 2 or part == 0:
                up[part] = ahead(up[part])
                out = put(out, up[part], chip - k, part)
            if k < CHIPS // 2 or part == 1:
                down[part] = behind(down[part])
                out = put(out, down[part], chip + k, part)
    return (out[None], incoming[None])


def solution(mesh):
    placed = (P("section", "tp", None, None), P("section", None, None))
    return jax.shard_map(
        shards,
        mesh=mesh,
        in_specs=placed,
        out_specs=(P("section", None, None), P("section", "tp", None)),
        check_vma=False,
    )
```

```python
import jax
import jax.numpy as jnp
import numpy as np
from jax import lax
from jax.experimental import pallas as pl
from jax.experimental.pallas import tpu as pltpu
from jax.sharding import PartitionSpec as P

BLOCK = 128
D = 16384
HALF = D // 2
PIECES = 2
COLS = HALF // PIECES
CHIPS = 8
FAR = CHIPS // 2
OWN = 8
GROUP = 2 * OWN
UNIT = 2048
VMEM = pl.BlockSpec(memory_space=pltpu.VMEM)
ANY = pl.BlockSpec(memory_space=pl.ANY)
GRANT = pltpu.CompilerParams(vmem_limit_bytes=16 * 2**20)


SMALL = pl.CostEstimate(flops=1, bytes_accessed=1, transcendentals=0)


def position():
    place = lax.axis_index("tp")
    core = lax.rem(place, 2)
    return place // 2, core, 1 - 2 * core


def chip_at(chip, offset):
    return lax.rem(chip + offset + CHIPS, CHIPS)


def hadamard():
    i = lax.broadcasted_iota(jnp.int32, (BLOCK, BLOCK), 0)
    j = lax.broadcasted_iota(jnp.int32, (BLOCK, BLOCK), 1)
    common = i & j
    common = common ^ (common >> 4)
    common = common ^ (common >> 2)
    common = common ^ (common >> 1)
    return (1 - 2 * (common & 1)).astype(jnp.float32).astype(jnp.bfloat16)


def small_limit(peak):
    target = peak * np.float32(1.5 * (1.0 - 2.0**-19) / 448.0 / 32.0)
    wide = target * np.float32(2.0**23 + 1.0)
    return wide - (wide - target)


def code(rotated):
    size = jnp.abs(rotated)
    limit = small_limit(jnp.max(size, axis=1, keepdims=True))
    nudged = rotated * np.float32(1.0 + 2.0**-20)
    wide = nudged * np.float32(2.0**20 + 1.0)
    wide = jnp.where(size < limit, limit * np.float32(1.5 * 2.0**19), wide)
    return wide - (wide - nudged)


def coded_half(held, slot, store):
    h = hadamard()
    for start in range(0, HALF, UNIT):
        cols = range(start, start + UNIT, BLOCK)
        x = jnp.concatenate([held[slot, :, b : b + BLOCK] for b in cols], axis=0)
        values = code(jnp.dot(x, h, preferred_element_type=jnp.float32))
        for i, b in enumerate(cols):
            at = slice(b % COLS, b % COLS + BLOCK)
            store(b // COLS, at, values[i * GROUP : (i + 1) * GROUP])


def code_group(held, group, out, first, halves):
    for i in range(halves):

        def store(piece, at, values, base=i * PIECES):
            out[base + piece, :, at] = values.astype(jnp.bfloat16)

        coded_half(held, 2 * group + (first + i) % 2, store)


def far_kernel(x_ref, stream_ref, keep, send, held, rows, arrived):
    chip, core, _ = position()
    far = chip_at(chip, FAR)

    def fetch(ref, group, half, target, slot):
        source = ref.at[
            pl.ds(pl.multiple_of(group * GROUP, GROUP), GROUP), half * HALF : (half + 1) * HALF
        ]
        return pltpu.make_async_copy(source, target, arrived.at[slot])

    copies = []
    for i in (4, 3, 5, 2, 6, 1, 7, 0):
        group = chip_at(chip, i)
        for half in range(2):
            copies.append(fetch(x_ref, group, half, held.at[2 * group + half], len(copies)))
    for half in range(2):
        copies.append(fetch(stream_ref, chip, half, rows.at[half], len(copies)))
    for copy in copies:
        copy.start()
    for copy in copies[:2]:
        copy.wait()
    code_group(held, far, keep, core, 1)
    code_group(held, far, send, 1 - core, 1)
    for copy in copies[2:]:
        copy.wait()


def code_far(local, stream):
    part = jax.ShapeDtypeStruct((PIECES, GROUP, COLS), jnp.bfloat16)
    whole = jax.ShapeDtypeStruct((2 * CHIPS, GROUP, HALF), jnp.bfloat16)
    rows = jax.ShapeDtypeStruct((2, GROUP, HALF), jnp.bfloat16)
    return pl.pallas_call(
        far_kernel,
        out_shape=(part, part, whole, rows),
        in_specs=[pl.BlockSpec(memory_space=pltpu.HBM)] * 2,
        out_specs=(VMEM,) * 4,
        scratch_shapes=[pltpu.SemaphoreType.DMA((2 * CHIPS + 2,))],
        compiler_params=GRANT,
        cost_estimate=SMALL,
    )(local, stream)


def code_kernel(k, held, keep, send):
    chip, core, way = position()
    code_group(held, chip_at(chip, way * k), keep, core, 2)
    code_group(held, chip_at(chip, -way * k), send, 1 - core, 2)


def code_rows(held, k, after):
    part = jax.ShapeDtypeStruct((2 * PIECES, GROUP, COLS), jnp.bfloat16)
    return pl.pallas_call(
        lambda held_ref, _, *refs: code_kernel(k, held_ref, *refs),
        out_shape=(part, part),
        in_specs=[VMEM, ANY],
        out_specs=(VMEM, VMEM),
        compiler_params=GRANT,
        cost_estimate=SMALL,
    )(held, after)


def own_kernel(held, stream, near_ref, send_ref, rows_ref):
    chip, core, _ = position()
    first = core == 0
    for half in range(2):

        def store(piece, at, values, half=half):
            top, low = values[:OWN], values[OWN:]
            mine = jnp.where(first, top, low).astype(jnp.bfloat16)
            theirs = jnp.where(first, low, top).astype(jnp.bfloat16)
            near_ref[((half + core) % 2) * PIECES + piece, :, at] = mine
            send_ref[((half + 1 - core) % 2) * PIECES + piece, :, at] = theirs

        coded_half(held, 2 * chip + half, store)
        for i in range(PIECES):
            rows = stream[half, :, i * COLS : (i + 1) * COLS].astype(jnp.float32)
            rows = jnp.where(first, rows[:OWN], rows[OWN:])
            rows_ref[((half + core) % 2) * PIECES + i] = rows.astype(jnp.bfloat16)


def own_rows(held, stream, after):
    part = jax.ShapeDtypeStruct((2 * PIECES, OWN, COLS), jnp.bfloat16)
    return pl.pallas_call(
        lambda held_ref, stream_ref, _, *refs: own_kernel(held_ref, stream_ref, *refs),
        out_shape=(part, part, part),
        in_specs=[VMEM, VMEM, ANY],
        out_specs=(VMEM,) * 3,
        compiler_params=GRANT,
        cost_estimate=SMALL,
    )(held, stream, after)


def add_kernel(i, keep, got, *rest):
    total = keep[i].astype(jnp.float32) + got[i].astype(jnp.float32)
    for arrived in rest[:-1]:
        total = total + arrived[...].astype(jnp.float32)
    rest[-1][...] = total.astype(jnp.bfloat16)


def add(i, keep, got, arrived):
    blocks = [keep, got] + ([] if arrived is None else [arrived])
    return pl.pallas_call(
        lambda *refs: add_kernel(i, *refs),
        out_shape=jax.ShapeDtypeStruct((GROUP, COLS), jnp.bfloat16),
        in_specs=[VMEM] * len(blocks),
        out_specs=VMEM,
        compiler_params=GRANT,
        cost_estimate=SMALL,
    )(*blocks)


def last_add_kernel(half, keep, got, arrived, same, cross):
    first = position()[1] == 0
    for j in range(PIECES):
        i = half * PIECES + j
        total = keep[i].astype(jnp.float32) + got[i].astype(jnp.float32)
        total = total + arrived[j][...].astype(jnp.float32)
        top, low = total[:OWN], total[OWN:]
        same[j] = jnp.where(first, top, low).astype(jnp.bfloat16)
        cross[j] = jnp.where(first, low, top).astype(jnp.bfloat16)


def last_add(half, keep, got, arrived):
    part = jax.ShapeDtypeStruct((PIECES, OWN, COLS), jnp.bfloat16)
    return pl.pallas_call(
        lambda *refs: last_add_kernel(
            half, refs[0], refs[1], refs[2:-2], *refs[-2:]
        ),
        out_shape=(part, part),
        in_specs=[VMEM] * (PIECES + 2),
        out_specs=(VMEM, VMEM),
        compiler_params=GRANT,
        cost_estimate=SMALL,
    )(keep, got, *arrived)


def norm_kernel(near, rows, got, same0, same1, cross0, cross1, hidden_ref, out0, out1):
    sames, crosses = (same0, same1), (cross1, cross0)
    f32 = jnp.float32
    squares = jnp.zeros((OWN, COLS), f32)
    for half in range(2):
        for j in range(PIECES):
            i = half * PIECES + j
            total = near[i].astype(f32) + got[i].astype(f32)
            total = total + sames[half][j].astype(f32) + crosses[half][j].astype(f32)
            hidden = rows[i].astype(f32) + total * np.float32(BLOCK**-0.5)
            hidden = hidden.astype(jnp.bfloat16)
            hidden_ref[i] = hidden
            hidden = hidden.astype(f32)
            squares = squares + hidden * hidden
    mean = jnp.sum(squares, axis=1, keepdims=True) / D
    inv_rms = lax.rsqrt(mean + np.float32(1e-05))
    for half, out in enumerate((out0, out1)):
        for j in range(PIECES):
            hidden = hidden_ref[half * PIECES + j].astype(f32)
            out[j] = (hidden * inv_rms).astype(jnp.bfloat16)


def norm(*blocks):
    part = jax.ShapeDtypeStruct((PIECES, OWN, COLS), jnp.bfloat16)
    return pl.pallas_call(
        norm_kernel,
        out_shape=(jax.ShapeDtypeStruct((2 * PIECES, OWN, COLS), jnp.bfloat16), part, part),
        in_specs=[VMEM] * len(blocks),
        out_specs=(VMEM,) * 3,
        compiler_params=GRANT,
        cost_estimate=SMALL,
    )(*blocks)


def join_kernel(count, *refs):
    at = 0
    for ref in refs[:count]:
        n = ref.shape[0]
        refs[-1][at : at + n] = ref[...]
        at += n


def join(blocks, after):
    n = sum(b.shape[0] for b in blocks)
    return pl.pallas_call(
        lambda *refs: join_kernel(len(blocks), *refs),
        out_shape=jax.ShapeDtypeStruct((n, OWN, COLS), jnp.bfloat16),
        in_specs=[VMEM] * len(blocks) + [ANY] * len(after),
        out_specs=VMEM,
        compiler_params=GRANT,
        cost_estimate=SMALL,
    )(*blocks, *after)


def put_kernel(places, aliased, *refs):
    sems, out, done = refs[-1], refs[-2], refs[-3]
    blocks = refs[aliased : aliased + len(places)]
    incoming = refs[-4]
    done[...] = jnp.zeros_like(done)
    chip, core, way = position()
    copies = []
    for block, held in zip(blocks, places):
        for i, (offset, rows, half) in enumerate(held):
            for j in range(PIECES):
                cols = pl.ds(pl.multiple_of(((core + half) % 2) * HALF + j * COLS, COLS), COLS)
                if offset is None:
                    target = incoming.at[0, :, cols]
                else:
                    owner = 2 * chip_at(chip, way * offset) + (core + rows) % 2
                    target = out.at[owner, :, cols]
                copies.append(
                    pltpu.make_async_copy(block.at[i * PIECES + j], target, sems.at[len(copies)])
                )
    for copy in copies:
        copy.start()
    for copy in copies:
        copy.wait()


def put(out, blocks, places):
    copies = PIECES * sum(len(p) for p in places)
    held = [] if out is None else [pltpu.with_memory_space_constraint(out, pltpu.HBM)]
    whole = pltpu.HBM((2 * CHIPS, OWN, D), jnp.bfloat16)
    rows = pltpu.HBM((1, OWN, D), jnp.bfloat16)
    done = jax.ShapeDtypeStruct((8, BLOCK), jnp.float32)
    with_rows = any(p[0] is None for held_places in places for p in held_places)
    outs = [rows, done, whole] if with_rows else [done, whole]
    space = pl.BlockSpec(memory_space=pltpu.HBM)
    return pl.pallas_call(
        lambda *refs: put_kernel(places, len(held), *refs),
        out_shape=outs,
        in_specs=[space] * len(held) + [VMEM] * len(blocks),
        out_specs=[space] * (len(outs) - 2) + [VMEM, space],
        scratch_shapes=[pltpu.SemaphoreType.DMA((copies,))],
        input_output_aliases={0: len(outs) - 1} if held else {},
        compiler_params=GRANT,
        cost_estimate=SMALL,
    )(*held, *blocks)


def shards(partials, residual):
    local = pltpu.with_memory_space_constraint(partials[0, 0], pltpu.HBM)
    stream = pltpu.with_memory_space_constraint(residual[0], pltpu.HBM)
    n = 2 * CHIPS

    def onward(block, cross=False):
        route = [(i, (i + 2 - 4 * (i % 2)) % n) for i in range(n)]
        return lax.ppermute(block, "tp", [(i, j ^ 1) if cross else (i, j) for i, j in route])

    def other_core(block):
        return lax.ppermute(block, "tp", [(i, i ^ 1) for i in range(n)])

    moving = [None] * (2 * PIECES)
    keep, send, held, rows = code_far(local, stream)
    for k in range(FAR, 1, -1):
        got = other_core(send)
        sums = [add(i, keep, got, moving[i]) for i in range(keep.shape[0])]
        keep, send = code_rows(held, k - 1, send)
        moving = [onward(block) for block in sums] + moving[len(sums) :]
    got = other_core(send)
    near, send, rows = own_rows(held, rows, send)
    same, cross = [], []
    for half in (0, 1):
        span = slice(half * PIECES, (half + 1) * PIECES)
        mine, theirs = last_add(half, keep, got, moving[span])
        same.append(onward(mine))
        cross.append(onward(theirs, True))
    hidden, *normed = norm(near, rows, other_core(send), *same, *cross)

    sections = lax.axis_size("section")
    theirs = [other_core(normed[1]), other_core(normed[0])]
    hidden = join([hidden], theirs[:1])
    incoming = lax.ppermute(hidden, "section", [(i, (i + 1) % sections) for i in range(sections)])

    moving = normed + theirs
    blocks = list(moving)
    places = [[(0, rows, half)] for rows in (0, 1) for half in (0, 1)]
    out = None
    joined, joined_places = [], []
    for k in range(1, FAR + 1):
        kept = [(rows, half) for rows in (0, 1) for half in (0, 1) if half == 0 or k < FAR]
        ready = [moving[2 * rows + half] for rows, half in kept]
        if k == 2:
            ready[-1] = join(ready[-1:], [incoming])
        moving = [onward(block) for block in ready]
        blocks += moving
        places += [[(-k, rows, half)] for rows, half in kept]
        if k == FAR - 1:
            blocks.append(incoming)
            places.append([(None, 0, 0), (None, 0, 1)])
            incoming, _, out = put(out, blocks, places)
            blocks, places = [], []
        joined += moving
        joined_places += [(k, 1 - rows, 1 - half) for rows, half in kept]
    blocks.append(other_core(join(joined, [])))
    places.append(joined_places)
    _, out = put(out, blocks, places)
    return (out.reshape(1, 2 * CHIPS * OWN, D), incoming)


def solution(mesh):
    placed = (P("section", "tp", None, None), P("section", None, None))
    return jax.shard_map(
        shards,
        mesh=mesh,
        in_specs=placed,
        out_specs=(P("section", None, None), P("section", "tp", None)),
        check_vma=False,
    )
```

```python
import jax
import jax.numpy as jnp
import numpy as np
from jax import lax
from jax.experimental import pallas as pl
from jax.experimental.pallas import tpu as pltpu
from jax.sharding import PartitionSpec as P

BLOCK = 128
D = 16384
HALF = D // 2
PIECES = 2
COLS = HALF // PIECES
CHIPS = 8
FAR = CHIPS // 2
OWN = 8
GROUP = 2 * OWN
UNIT = 2048
VMEM = pl.BlockSpec(memory_space=pltpu.VMEM)
ANY = pl.BlockSpec(memory_space=pl.ANY)
GRANT = pltpu.CompilerParams(vmem_limit_bytes=16 * 2**20)


SMALL = pl.CostEstimate(flops=1, bytes_accessed=1, transcendentals=0)


def position():
    place = lax.axis_index("tp")
    core = lax.rem(place, 2)
    return place // 2, core, 1 - 2 * core


def chip_at(chip, offset):
    return lax.rem(chip + offset + CHIPS, CHIPS)


def hadamard():
    i = lax.broadcasted_iota(jnp.int32, (BLOCK, BLOCK), 0)
    j = lax.broadcasted_iota(jnp.int32, (BLOCK, BLOCK), 1)
    common = i & j
    common = common ^ (common >> 4)
    common = common ^ (common >> 2)
    common = common ^ (common >> 1)
    return (1 - 2 * (common & 1)).astype(jnp.float32).astype(jnp.bfloat16)


def small_limit(peak):
    target = peak * np.float32(1.5 * (1.0 - 2.0**-19) / 448.0 / 32.0)
    wide = target * np.float32(2.0**23 + 1.0)
    return wide - (wide - target)


def code(rotated):
    size = jnp.abs(rotated)
    limit = small_limit(jnp.max(size, axis=1, keepdims=True))
    nudged = rotated * np.float32(1.0 + 2.0**-20)
    wide = nudged * np.float32(2.0**20 + 1.0)
    wide = jnp.where(size < limit, limit * np.float32(1.5 * 2.0**19), wide)
    return wide - (wide - nudged)


def coded_half(held, slot, store):
    h = hadamard()
    for start in range(0, HALF, UNIT):
        cols = range(start, start + UNIT, BLOCK)
        x = jnp.concatenate([held[slot, :, b : b + BLOCK] for b in cols], axis=0)
        values = code(jnp.dot(x, h, preferred_element_type=jnp.float32))
        for i, b in enumerate(cols):
            at = slice(b % COLS, b % COLS + BLOCK)
            store(b // COLS, at, values[i * GROUP : (i + 1) * GROUP])


def code_group(held, group, out, first, halves):
    for i in range(halves):

        def store(piece, at, values, base=i * PIECES):
            out[base + piece, :, at] = values.astype(jnp.bfloat16)

        coded_half(held, 2 * group + (first + i) % 2, store)


def far_kernel(x_ref, stream_ref, keep, send, held, rows, arrived):
    chip, core, _ = position()
    far = chip_at(chip, FAR)

    def fetch(ref, group, half, target, slot):
        source = ref.at[
            pl.ds(pl.multiple_of(group * GROUP, GROUP), GROUP), half * HALF : (half + 1) * HALF
        ]
        return pltpu.make_async_copy(source, target, arrived.at[slot])

    copies = []
    for i in (4, 3, 5, 2, 6, 1, 7, 0):
        group = chip_at(chip, i)
        for half in range(2):
            copies.append(fetch(x_ref, group, half, held.at[2 * group + half], len(copies)))
    for half in range(2):
        copies.append(fetch(stream_ref, chip, half, rows.at[half], len(copies)))
    for copy in copies:
        copy.start()
    for copy in copies[:2]:
        copy.wait()
    code_group(held, far, keep, core, 1)
    code_group(held, far, send, 1 - core, 1)
    for copy in copies[2:]:
        copy.wait()


def code_far(local, stream):
    part = jax.ShapeDtypeStruct((PIECES, GROUP, COLS), jnp.bfloat16)
    whole = jax.ShapeDtypeStruct((2 * CHIPS, GROUP, HALF), jnp.bfloat16)
    rows = jax.ShapeDtypeStruct((2, GROUP, HALF), jnp.bfloat16)
    return pl.pallas_call(
        far_kernel,
        out_shape=(part, part, whole, rows),
        in_specs=[pl.BlockSpec(memory_space=pltpu.HBM)] * 2,
        out_specs=(VMEM,) * 4,
        scratch_shapes=[pltpu.SemaphoreType.DMA((2 * CHIPS + 2,))],
        compiler_params=GRANT,
        cost_estimate=SMALL,
    )(local, stream)


def code_kernel(k, held, keep, send):
    chip, core, way = position()
    code_group(held, chip_at(chip, way * k), keep, core, 2)
    code_group(held, chip_at(chip, -way * k), send, 1 - core, 2)


def code_rows(held, k, after):
    part = jax.ShapeDtypeStruct((2 * PIECES, GROUP, COLS), jnp.bfloat16)
    return pl.pallas_call(
        lambda held_ref, _, *refs: code_kernel(k, held_ref, *refs),
        out_shape=(part, part),
        in_specs=[VMEM, ANY],
        out_specs=(VMEM, VMEM),
        compiler_params=GRANT,
        cost_estimate=SMALL,
    )(held, after)


def own_kernel(held, stream, near_ref, send_ref, rows_ref):
    chip, core, _ = position()
    first = core == 0
    for half in range(2):

        def store(piece, at, values, half=half):
            top, low = values[:OWN], values[OWN:]
            mine = jnp.where(first, top, low).astype(jnp.bfloat16)
            theirs = jnp.where(first, low, top).astype(jnp.bfloat16)
            near_ref[((half + core) % 2) * PIECES + piece, :, at] = mine
            send_ref[((half + 1 - core) % 2) * PIECES + piece, :, at] = theirs

        coded_half(held, 2 * chip + half, store)
        for i in range(PIECES):
            rows = stream[half, :, i * COLS : (i + 1) * COLS].astype(jnp.float32)
            rows = jnp.where(first, rows[:OWN], rows[OWN:])
            rows_ref[((half + core) % 2) * PIECES + i] = rows.astype(jnp.bfloat16)


def own_rows(held, stream, after):
    part = jax.ShapeDtypeStruct((2 * PIECES, OWN, COLS), jnp.bfloat16)
    return pl.pallas_call(
        lambda held_ref, stream_ref, _, *refs: own_kernel(held_ref, stream_ref, *refs),
        out_shape=(part, part, part),
        in_specs=[VMEM, VMEM, ANY],
        out_specs=(VMEM,) * 3,
        compiler_params=GRANT,
        cost_estimate=SMALL,
    )(held, stream, after)


def add_kernel(i, keep, got, *rest):
    total = keep[i].astype(jnp.float32) + got[i].astype(jnp.float32)
    for arrived in rest[:-1]:
        total = total + arrived[...].astype(jnp.float32)
    rest[-1][...] = total.astype(jnp.bfloat16)


def add(i, keep, got, arrived):
    blocks = [keep, got] + ([] if arrived is None else [arrived])
    return pl.pallas_call(
        lambda *refs: add_kernel(i, *refs),
        out_shape=jax.ShapeDtypeStruct((GROUP, COLS), jnp.bfloat16),
        in_specs=[VMEM] * len(blocks),
        out_specs=VMEM,
        compiler_params=GRANT,
        cost_estimate=SMALL,
    )(*blocks)


def last_add_kernel(half, keep, got, arrived, same, cross):
    first = position()[1] == 0
    for j in range(PIECES):
        i = half * PIECES + j
        total = keep[i].astype(jnp.float32) + got[i].astype(jnp.float32)
        total = total + arrived[j][...].astype(jnp.float32)
        top, low = total[:OWN], total[OWN:]
        same[j] = jnp.where(first, top, low).astype(jnp.bfloat16)
        cross[j] = jnp.where(first, low, top).astype(jnp.bfloat16)


def last_add(half, keep, got, arrived):
    part = jax.ShapeDtypeStruct((PIECES, OWN, COLS), jnp.bfloat16)
    return pl.pallas_call(
        lambda *refs: last_add_kernel(
            half, refs[0], refs[1], refs[2:-2], *refs[-2:]
        ),
        out_shape=(part, part),
        in_specs=[VMEM] * (PIECES + 2),
        out_specs=(VMEM, VMEM),
        compiler_params=GRANT,
        cost_estimate=SMALL,
    )(keep, got, *arrived)


def norm_kernel(near, rows, got, same0, same1, cross0, cross1, hidden_ref, whole, out0, out1):
    sames, crosses = (same0, same1), (cross1, cross0)
    f32 = jnp.float32
    squares = jnp.zeros((OWN, COLS), f32)
    for half in range(2):
        for j in range(PIECES):
            i = half * PIECES + j
            total = near[i].astype(f32) + got[i].astype(f32)
            total = total + sames[half][j].astype(f32) + crosses[half][j].astype(f32)
            hidden = rows[i].astype(f32) + total * np.float32(BLOCK**-0.5)
            hidden = hidden.astype(jnp.bfloat16)
            hidden_ref[i] = hidden
            hidden = hidden.astype(f32)
            squares = squares + hidden * hidden
    mean = jnp.sum(squares, axis=1, keepdims=True) / D
    inv_rms = lax.rsqrt(mean + np.float32(1e-05))
    for half, out in enumerate((out0, out1)):
        for j in range(PIECES):
            hidden = hidden_ref[half * PIECES + j].astype(f32)
            normed = (hidden * inv_rms).astype(jnp.bfloat16)
            out[j] = normed
            whole[half * PIECES + j] = normed


def norm(*blocks):
    part = jax.ShapeDtypeStruct((PIECES, OWN, COLS), jnp.bfloat16)
    return pl.pallas_call(
        norm_kernel,
        out_shape=(jax.ShapeDtypeStruct((2 * PIECES, OWN, COLS), jnp.bfloat16),) * 2 + (part, part),
        in_specs=[VMEM] * len(blocks),
        out_specs=(VMEM,) * 4,
        compiler_params=GRANT,
        cost_estimate=SMALL,
    )(*blocks)


def split_kernel(block, low, high):
    low[...] = block[:PIECES]
    high[...] = block[PIECES:]


def split(block):
    part = jax.ShapeDtypeStruct((PIECES, OWN, COLS), jnp.bfloat16)
    return pl.pallas_call(
        split_kernel,
        out_shape=(part, part),
        in_specs=[VMEM],
        out_specs=(VMEM, VMEM),
        compiler_params=GRANT,
        cost_estimate=SMALL,
    )(block)


def join_kernel(count, *refs):
    at = 0
    for ref in refs[:count]:
        n = ref.shape[0]
        refs[-1][at : at + n] = ref[...]
        at += n


def join(blocks, after):
    n = sum(b.shape[0] for b in blocks)
    return pl.pallas_call(
        lambda *refs: join_kernel(len(blocks), *refs),
        out_shape=jax.ShapeDtypeStruct((n, OWN, COLS), jnp.bfloat16),
        in_specs=[VMEM] * len(blocks) + [ANY] * len(after),
        out_specs=VMEM,
        compiler_params=GRANT,
        cost_estimate=SMALL,
    )(*blocks, *after)


def put_kernel(places, aliased, *refs):
    sems, out, done = refs[-1], refs[-2], refs[-3]
    blocks = refs[aliased : aliased + len(places)]
    incoming = refs[-4]
    done[...] = jnp.zeros_like(done)
    chip, core, way = position()
    copies = []
    for block, held in zip(blocks, places):
        for i, (offset, rows, half) in enumerate(held):
            for j in range(PIECES):
                cols = pl.ds(pl.multiple_of(((core + half) % 2) * HALF + j * COLS, COLS), COLS)
                if offset is None:
                    target = incoming.at[0, :, cols]
                else:
                    owner = 2 * chip_at(chip, way * offset) + (core + rows) % 2
                    target = out.at[owner, :, cols]
                copies.append(
                    pltpu.make_async_copy(block.at[i * PIECES + j], target, sems.at[len(copies)])
                )
    for copy in copies:
        copy.start()
    for copy in copies:
        copy.wait()


def put(out, blocks, places, after):
    copies = PIECES * sum(len(p) for p in places)
    held = [] if out is None else [pltpu.with_memory_space_constraint(out, pltpu.HBM)]
    whole = pltpu.HBM((2 * CHIPS, OWN, D), jnp.bfloat16)
    rows = pltpu.HBM((1, OWN, D), jnp.bfloat16)
    done = jax.ShapeDtypeStruct((8, BLOCK), jnp.float32)
    with_rows = any(p[0] is None for held_places in places for p in held_places)
    outs = [rows, done, whole] if with_rows else [done, whole]
    space = pl.BlockSpec(memory_space=pltpu.HBM)
    return pl.pallas_call(
        lambda *refs: put_kernel(places, len(held) + len(after), *refs),
        out_shape=outs,
        in_specs=[space] * len(held) + [ANY] * len(after) + [VMEM] * len(blocks),
        out_specs=[space] * (len(outs) - 2) + [VMEM, space],
        scratch_shapes=[pltpu.SemaphoreType.DMA((copies,))],
        input_output_aliases={0: len(outs) - 1} if held else {},
        compiler_params=GRANT,
        cost_estimate=SMALL,
    )(*held, *after, *blocks)


def shards(partials, residual):
    local = pltpu.with_memory_space_constraint(partials[0, 0], pltpu.HBM)
    stream = pltpu.with_memory_space_constraint(residual[0], pltpu.HBM)
    n = 2 * CHIPS

    def onward(block, cross=False):
        route = [(i, (i + 2 - 4 * (i % 2)) % n) for i in range(n)]
        return lax.ppermute(block, "tp", [(i, j ^ 1) if cross else (i, j) for i, j in route])

    def other_core(block):
        return lax.ppermute(block, "tp", [(i, i ^ 1) for i in range(n)])

    moving = [None] * (2 * PIECES)
    keep, send, held, rows = code_far(local, stream)
    for k in range(FAR, 1, -1):
        got = other_core(send)
        order = [i for i in (0, 1, 2, 3) if i < keep.shape[0]]
        sums = {i: add(i, keep, got, moving[i]) for i in order}
        keep, send = code_rows(held, k - 1, send)
        for i in order:
            moving[i] = onward(sums[i])
    got = other_core(send)
    near, send, rows = own_rows(held, rows, send)
    same, cross = [], []
    for half in (0, 1):
        span = slice(half * PIECES, (half + 1) * PIECES)
        mine, theirs = last_add(half, keep, got, moving[span])
        same.append(onward(mine))
        cross.append(onward(theirs, True))
    hidden, whole, *normed = norm(near, rows, other_core(send), *same, *cross)

    sections = lax.axis_size("section")
    theirs = list(split(other_core(whole)))[::-1]

    moving = normed + theirs
    blocks = list(moving)
    places = [[(0, rows, half)] for rows in (0, 1) for half in (0, 1)]
    joined, joined_places = [], []
    for k in range(1, FAR + 1):
        kept = [(rows, half) for rows, half in [(0, 0), (0, 1), (1, 0), (1, 1)] if half == 0 or k < FAR]
        ready = [moving[2 * rows + half] for rows, half in kept]
        if k == FAR:
            ready[-1] = join(ready[-1:], [incoming])
        for (rows, half), block in zip(kept, ready):
            moving[2 * rows + half] = onward(block)
        arrived = [moving[2 * rows + half] for rows, half in kept]
        if k == 1:
            hidden = join([hidden], arrived[2:3])
            incoming = lax.ppermute(
                hidden, "section", [(i, (i + 1) % sections) for i in range(sections)]
            )
        if k == FAR:
            swapped = other_core(join(joined[:8], []))
            swapped_places, joined, joined_places = joined_places[:8], joined[8:], joined_places[8:]
            early = put(None, blocks, places, arrived[:1])
            blocks, places = late, late_places
        joined += arrived
        joined_places += [(k, 1 - rows, 1 - half) for rows, half in kept]
        if k < FAR - 1:
            blocks += arrived
            places += [[(-k, rows, half)] for rows, half in kept]
            if k == 1:
                blocks.append(incoming)
                places.append([(None, 0, 0), (None, 0, 1)])
            late, late_places = [], []
        else:
            late += arrived
            late_places += [[(-k, rows, half)] for rows, half in kept]
    incoming, token, out = early
    last = other_core(join(joined, [token]))
    _, out = put(out, blocks + [swapped], places + [swapped_places], [])
    _, out = put(out, [last], [joined_places], [])
    return (out.reshape(1, 2 * CHIPS * OWN, D), incoming)


def solution(mesh):
    placed = (P("section", "tp", None, None), P("section", None, None))
    return jax.shard_map(
        shards,
        mesh=mesh,
        in_specs=placed,
        out_specs=(P("section", None, None), P("section", "tp", None)),
        check_vma=False,
    )
```

```python
import jax
import jax.numpy as jnp
import numpy as np
from jax import lax
from jax.experimental import pallas as pl
from jax.experimental.pallas import tpu as pltpu
from jax.sharding import PartitionSpec as P

BLOCK = 128
D = 16384
HALF = D // 2
PIECES = 1
COLS = HALF // PIECES
CHIPS = 8
FAR = CHIPS // 2
OWN = 8
GROUP = 2 * OWN
UNIT = 2048
VMEM = pl.BlockSpec(memory_space=pltpu.VMEM)
ANY = pl.BlockSpec(memory_space=pl.ANY)
GRANT = pltpu.CompilerParams(vmem_limit_bytes=16 * 2**20)


SMALL = pl.CostEstimate(flops=1, bytes_accessed=1, transcendentals=0)


def position():
    place = lax.axis_index("tp")
    core = lax.rem(place, 2)
    return place // 2, core, 1 - 2 * core


def chip_at(chip, offset):
    return lax.rem(chip + offset + CHIPS, CHIPS)


def hadamard():
    i = lax.broadcasted_iota(jnp.int32, (BLOCK, BLOCK), 0)
    j = lax.broadcasted_iota(jnp.int32, (BLOCK, BLOCK), 1)
    common = i & j
    common = common ^ (common >> 4)
    common = common ^ (common >> 2)
    common = common ^ (common >> 1)
    return (1 - 2 * (common & 1)).astype(jnp.float32).astype(jnp.bfloat16)


def small_limit(peak):
    target = peak * np.float32(1.5 * (1.0 - 2.0**-19) / 448.0 / 32.0)
    wide = target * np.float32(2.0**23 + 1.0)
    return wide - (wide - target)


def code(rotated):
    size = jnp.abs(rotated)
    limit = small_limit(jnp.max(size, axis=1, keepdims=True))
    nudged = rotated * np.float32(1.0 + 2.0**-20)
    wide = nudged * np.float32(2.0**20 + 1.0)
    wide = jnp.where(size < limit, limit * np.float32(1.5 * 2.0**19), wide)
    return wide - (wide - nudged)


def coded_half(held, slot, store):
    h = hadamard()
    for start in range(0, HALF, UNIT):
        cols = range(start, start + UNIT, BLOCK)
        x = jnp.concatenate([held[slot, :, b : b + BLOCK] for b in cols], axis=0)
        values = code(jnp.dot(x, h, preferred_element_type=jnp.float32))
        for i, b in enumerate(cols):
            at = slice(b % COLS, b % COLS + BLOCK)
            store(b // COLS, at, values[i * GROUP : (i + 1) * GROUP])


def code_group(held, group, out, first, halves):
    for i in range(halves):

        def store(piece, at, values, base=i * PIECES):
            out[base + piece, :, at] = values.astype(jnp.bfloat16)

        coded_half(held, 2 * group + (first + i) % 2, store)


def far_kernel(x_ref, stream_ref, keep, send, held, rows, arrived):
    chip, core, _ = position()
    far = chip_at(chip, FAR)

    def fetch(ref, group, half, target, slot):
        source = ref.at[
            pl.ds(pl.multiple_of(group * GROUP, GROUP), GROUP), half * HALF : (half + 1) * HALF
        ]
        return pltpu.make_async_copy(source, target, arrived.at[slot])

    copies = []
    for i in (4, 3, 5, 2, 6, 1, 7, 0):
        group = chip_at(chip, i)
        for half in range(2):
            copies.append(fetch(x_ref, group, half, held.at[2 * group + half], len(copies)))
    for half in range(2):
        copies.append(fetch(stream_ref, chip, half, rows.at[half], len(copies)))
    for copy in copies:
        copy.start()
    for copy in copies[:2]:
        copy.wait()
    code_group(held, far, keep, core, 1)
    code_group(held, far, send, 1 - core, 1)
    for copy in copies[2:]:
        copy.wait()


def code_far(local, stream):
    part = jax.ShapeDtypeStruct((PIECES, GROUP, COLS), jnp.bfloat16)
    whole = jax.ShapeDtypeStruct((2 * CHIPS, GROUP, HALF), jnp.bfloat16)
    rows = jax.ShapeDtypeStruct((2, GROUP, HALF), jnp.bfloat16)
    return pl.pallas_call(
        far_kernel,
        out_shape=(part, part, whole, rows),
        in_specs=[pl.BlockSpec(memory_space=pltpu.HBM)] * 2,
        out_specs=(VMEM,) * 4,
        scratch_shapes=[pltpu.SemaphoreType.DMA((2 * CHIPS + 2,))],
        compiler_params=GRANT,
        cost_estimate=SMALL,
    )(local, stream)


def code_kernel(k, held, keep, send):
    chip, core, way = position()
    code_group(held, chip_at(chip, way * k), keep, core, 2)
    code_group(held, chip_at(chip, -way * k), send, 1 - core, 2)


def code_rows(held, k, after):
    part = jax.ShapeDtypeStruct((2 * PIECES, GROUP, COLS), jnp.bfloat16)
    return pl.pallas_call(
        lambda held_ref, _, *refs: code_kernel(k, held_ref, *refs),
        out_shape=(part, part),
        in_specs=[VMEM, ANY],
        out_specs=(VMEM, VMEM),
        compiler_params=GRANT,
        cost_estimate=SMALL,
    )(held, after)


def own_kernel(held, stream, near_ref, send_ref, rows_ref):
    chip, core, _ = position()
    first = core == 0
    for half in range(2):

        def store(piece, at, values, half=half):
            top, low = values[:OWN], values[OWN:]
            mine = jnp.where(first, top, low).astype(jnp.bfloat16)
            theirs = jnp.where(first, low, top).astype(jnp.bfloat16)
            near_ref[((half + core) % 2) * PIECES + piece, :, at] = mine
            send_ref[((half + 1 - core) % 2) * PIECES + piece, :, at] = theirs

        coded_half(held, 2 * chip + half, store)
        for i in range(PIECES):
            rows = stream[half, :, i * COLS : (i + 1) * COLS].astype(jnp.float32)
            rows = jnp.where(first, rows[:OWN], rows[OWN:])
            rows_ref[((half + core) % 2) * PIECES + i] = rows.astype(jnp.bfloat16)


def own_rows(held, stream, after):
    part = jax.ShapeDtypeStruct((2 * PIECES, OWN, COLS), jnp.bfloat16)
    return pl.pallas_call(
        lambda held_ref, stream_ref, _, *refs: own_kernel(held_ref, stream_ref, *refs),
        out_shape=(part, part, part),
        in_specs=[VMEM, VMEM, ANY],
        out_specs=(VMEM,) * 3,
        compiler_params=GRANT,
        cost_estimate=SMALL,
    )(held, stream, after)


def add_kernel(i, keep, got, *rest):
    total = keep[i].astype(jnp.float32) + got[i].astype(jnp.float32)
    for arrived in rest[:-1]:
        total = total + arrived[...].astype(jnp.float32)
    rest[-1][...] = total.astype(jnp.bfloat16)


def add(i, keep, got, arrived):
    blocks = [keep, got] + ([] if arrived is None else [arrived])
    return pl.pallas_call(
        lambda *refs: add_kernel(i, *refs),
        out_shape=jax.ShapeDtypeStruct((GROUP, COLS), jnp.bfloat16),
        in_specs=[VMEM] * len(blocks),
        out_specs=VMEM,
        compiler_params=GRANT,
        cost_estimate=SMALL,
    )(*blocks)


def last_add_kernel(half, keep, got, arrived, same, cross):
    first = position()[1] == 0
    for j in range(PIECES):
        i = half * PIECES + j
        total = keep[i].astype(jnp.float32) + got[i].astype(jnp.float32)
        total = total + arrived[j][...].astype(jnp.float32)
        top, low = total[:OWN], total[OWN:]
        same[j] = jnp.where(first, top, low).astype(jnp.bfloat16)
        cross[j] = jnp.where(first, low, top).astype(jnp.bfloat16)


def last_add(half, keep, got, arrived):
    part = jax.ShapeDtypeStruct((PIECES, OWN, COLS), jnp.bfloat16)
    return pl.pallas_call(
        lambda *refs: last_add_kernel(
            half, refs[0], refs[1], refs[2:-2], *refs[-2:]
        ),
        out_shape=(part, part),
        in_specs=[VMEM] * (PIECES + 2),
        out_specs=(VMEM, VMEM),
        compiler_params=GRANT,
        cost_estimate=SMALL,
    )(keep, got, *arrived)


def norm_kernel(near, rows, got, same0, same1, cross0, cross1, hidden_ref, whole, out0, out1):
    sames, crosses = (same0, same1), (cross1, cross0)
    f32 = jnp.float32
    squares = jnp.zeros((OWN, COLS), f32)
    for half in range(2):
        for j in range(PIECES):
            i = half * PIECES + j
            total = near[i].astype(f32) + got[i].astype(f32)
            total = total + sames[half][j].astype(f32) + crosses[half][j].astype(f32)
            hidden = rows[i].astype(f32) + total * np.float32(BLOCK**-0.5)
            hidden = hidden.astype(jnp.bfloat16)
            hidden_ref[i] = hidden
            hidden = hidden.astype(f32)
            squares = squares + hidden * hidden
    mean = jnp.sum(squares, axis=1, keepdims=True) / D
    inv_rms = lax.rsqrt(mean + np.float32(1e-05))
    for half, out in enumerate((out0, out1)):
        for j in range(PIECES):
            hidden = hidden_ref[half * PIECES + j].astype(f32)
            normed = (hidden * inv_rms).astype(jnp.bfloat16)
            out[j] = normed
            whole[half * PIECES + j] = normed


def norm(*blocks):
    part = jax.ShapeDtypeStruct((PIECES, OWN, COLS), jnp.bfloat16)
    return pl.pallas_call(
        norm_kernel,
        out_shape=(jax.ShapeDtypeStruct((2 * PIECES, OWN, COLS), jnp.bfloat16),) * 2 + (part, part),
        in_specs=[VMEM] * len(blocks),
        out_specs=(VMEM,) * 4,
        compiler_params=GRANT,
        cost_estimate=SMALL,
    )(*blocks)


def split_kernel(block, low, high):
    low[...] = block[:PIECES]
    high[...] = block[PIECES:]


def split(block):
    part = jax.ShapeDtypeStruct((PIECES, OWN, COLS), jnp.bfloat16)
    return pl.pallas_call(
        split_kernel,
        out_shape=(part, part),
        in_specs=[VMEM],
        out_specs=(VMEM, VMEM),
        compiler_params=GRANT,
        cost_estimate=SMALL,
    )(block)


def join_kernel(count, *refs):
    at = 0
    for ref in refs[:count]:
        n = ref.shape[0]
        refs[-1][at : at + n] = ref[...]
        at += n


def join(blocks, after):
    n = sum(b.shape[0] for b in blocks)
    return pl.pallas_call(
        lambda *refs: join_kernel(len(blocks), *refs),
        out_shape=jax.ShapeDtypeStruct((n, OWN, COLS), jnp.bfloat16),
        in_specs=[VMEM] * len(blocks) + [ANY] * len(after),
        out_specs=VMEM,
        compiler_params=GRANT,
        cost_estimate=SMALL,
    )(*blocks, *after)


def put_kernel(places, aliased, *refs):
    sems, out, done = refs[-1], refs[-2], refs[-3]
    blocks = refs[aliased : aliased + len(places)]
    incoming = refs[-4]
    done[...] = jnp.zeros_like(done)
    chip, core, way = position()
    copies = []
    for block, held in zip(blocks, places):
        for i, (offset, rows, half) in enumerate(held):
            for j in range(PIECES):
                cols = pl.ds(pl.multiple_of(((core + half) % 2) * HALF + j * COLS, COLS), COLS)
                if offset is None:
                    target = incoming.at[0, :, cols]
                else:
                    owner = 2 * chip_at(chip, way * offset) + (core + rows) % 2
                    target = out.at[owner, :, cols]
                copies.append(
                    pltpu.make_async_copy(block.at[i * PIECES + j], target, sems.at[len(copies)])
                )
    for copy in copies:
        copy.start()
    for copy in copies:
        copy.wait()


def put(out, blocks, places, after):
    copies = PIECES * sum(len(p) for p in places)
    held = [] if out is None else [pltpu.with_memory_space_constraint(out, pltpu.HBM)]
    whole = pltpu.HBM((2 * CHIPS, OWN, D), jnp.bfloat16)
    rows = pltpu.HBM((1, OWN, D), jnp.bfloat16)
    done = jax.ShapeDtypeStruct((8, BLOCK), jnp.float32)
    with_rows = any(p[0] is None for held_places in places for p in held_places)
    outs = [rows, done, whole] if with_rows else [done, whole]
    space = pl.BlockSpec(memory_space=pltpu.HBM)
    return pl.pallas_call(
        lambda *refs: put_kernel(places, len(held) + len(after), *refs),
        out_shape=outs,
        in_specs=[space] * len(held) + [ANY] * len(after) + [VMEM] * len(blocks),
        out_specs=[space] * (len(outs) - 2) + [VMEM, space],
        scratch_shapes=[pltpu.SemaphoreType.DMA((copies,))],
        input_output_aliases={0: len(outs) - 1} if held else {},
        compiler_params=GRANT,
        cost_estimate=SMALL,
    )(*held, *after, *blocks)


def shards(partials, residual):
    local = pltpu.with_memory_space_constraint(partials[0, 0], pltpu.HBM)
    stream = pltpu.with_memory_space_constraint(residual[0], pltpu.HBM)
    n = 2 * CHIPS

    def onward(block, cross=False):
        route = [(i, (i + 2 - 4 * (i % 2)) % n) for i in range(n)]
        return lax.ppermute(block, "tp", [(i, j ^ 1) if cross else (i, j) for i, j in route])

    def other_core(block):
        return lax.ppermute(block, "tp", [(i, i ^ 1) for i in range(n)])

    moving = [None] * (2 * PIECES)
    keep, send, held, rows = code_far(local, stream)
    for k in range(FAR, 1, -1):
        got = other_core(send)
        order = [i for i in (0, 1, 2, 3) if i < keep.shape[0]]
        sums = {i: add(i, keep, got, moving[i]) for i in order}
        keep, send = code_rows(held, k - 1, send)
        for i in order:
            moving[i] = onward(sums[i])
    got = other_core(send)
    near, send, rows = own_rows(held, rows, send)
    same, cross = [], []
    for half in (0, 1):
        span = slice(half * PIECES, (half + 1) * PIECES)
        mine, theirs = last_add(half, keep, got, moving[span])
        same.append(onward(mine))
        cross.append(onward(theirs, True))
    hidden, whole, *normed = norm(near, rows, other_core(send), *same, *cross)

    sections = lax.axis_size("section")
    theirs = list(split(other_core(whole)))[::-1]

    moving = normed + theirs
    blocks = list(moving)
    places = [[(0, rows, half)] for rows in (0, 1) for half in (0, 1)]
    joined, joined_places = [], []
    for k in range(1, FAR + 1):
        kept = [(rows, half) for rows, half in [(0, 0), (0, 1), (1, 0), (1, 1)] if half == 0 or k < FAR]
        ready = [moving[2 * rows + half] for rows, half in kept]
        if k == FAR:
            ready[-1] = join(ready[-1:], [incoming])
        for (rows, half), block in zip(kept, ready):
            moving[2 * rows + half] = onward(block)
        arrived = [moving[2 * rows + half] for rows, half in kept]
        if k == 1:
            hidden = join([hidden], arrived[2:3])
            incoming = lax.ppermute(
                hidden, "section", [(i, (i + 1) % sections) for i in range(sections)]
            )
        if k == FAR:
            swapped = other_core(join(joined[:8], []))
            swapped_places, joined, joined_places = joined_places[:8], joined[8:], joined_places[8:]
            early = put(None, blocks, places, arrived[:1])
            blocks, places = late, late_places
        joined += arrived
        joined_places += [(k, 1 - rows, 1 - half) for rows, half in kept]
        if k < FAR - 1:
            blocks += arrived
            places += [[(-k, rows, half)] for rows, half in kept]
            if k == 1:
                blocks.append(incoming)
                places.append([(None, 0, 0), (None, 0, 1)])
            late, late_places = [], []
        else:
            late += arrived
            late_places += [[(-k, rows, half)] for rows, half in kept]
    incoming, token, out = early
    last = other_core(join(joined, [token]))
    _, out = put(out, blocks + [swapped], places + [swapped_places], [])
    _, out = put(out, [last], [joined_places], [])
    return (out.reshape(1, 2 * CHIPS * OWN, D), incoming)


def solution(mesh):
    placed = (P("section", "tp", None, None), P("section", None, None))
    return jax.shard_map(
        shards,
        mesh=mesh,
        in_specs=placed,
        out_specs=(P("section", None, None), P("section", "tp", None)),
        check_vma=False,
    )
```

```python
import jax
import jax.numpy as jnp
import numpy as np
from jax import lax
from jax.experimental import pallas as pl
from jax.experimental.pallas import tpu as pltpu
from jax.sharding import PartitionSpec as P

BLOCK = 128
D = 16384
HALF = D // 2
PIECES = 1
COLS = HALF // PIECES
CHIPS = 8
FAR = CHIPS // 2
OWN = 8
GROUP = 2 * OWN
UNIT = 2048
VMEM = pl.BlockSpec(memory_space=pltpu.VMEM)
ANY = pl.BlockSpec(memory_space=pl.ANY)
GRANT = pltpu.CompilerParams(vmem_limit_bytes=16 * 2**20)


SMALL = pl.CostEstimate(flops=1, bytes_accessed=1, transcendentals=0)


def position():
    place = lax.axis_index("tp")
    core = lax.rem(place, 2)
    return place // 2, core, 1 - 2 * core


def chip_at(chip, offset):
    return lax.rem(chip + offset + CHIPS, CHIPS)


def hadamard():
    i = lax.broadcasted_iota(jnp.int32, (BLOCK, BLOCK), 0)
    j = lax.broadcasted_iota(jnp.int32, (BLOCK, BLOCK), 1)
    common = i & j
    common = common ^ (common >> 4)
    common = common ^ (common >> 2)
    common = common ^ (common >> 1)
    return (1 - 2 * (common & 1)).astype(jnp.float32).astype(jnp.bfloat16)


def small_limit(peak):
    target = peak * np.float32(1.5 * (1.0 - 2.0**-19) / 448.0 / 32.0)
    wide = target * np.float32(2.0**23 + 1.0)
    return wide - (wide - target)


def code(rotated):
    size = jnp.abs(rotated)
    limit = small_limit(jnp.max(size, axis=1, keepdims=True))
    nudged = rotated * np.float32(1.0 + 2.0**-20)
    wide = nudged * np.float32(2.0**20 + 1.0)
    wide = jnp.where(size < limit, limit * np.float32(1.5 * 2.0**19), wide)
    return wide - (wide - nudged)


def coded_half(h, held, slot, store):
    for start in range(0, HALF, UNIT):
        cols = range(start, start + UNIT, BLOCK)
        x = jnp.concatenate([held[slot, :, b : b + BLOCK] for b in cols], axis=0)
        values = code(jnp.dot(x, h, preferred_element_type=jnp.float32))
        for i, b in enumerate(cols):
            at = slice(b % COLS, b % COLS + BLOCK)
            store(b // COLS, at, values[i * GROUP : (i + 1) * GROUP])


def code_group(h, held, group, out, first, halves):
    for i in range(halves):

        def store(piece, at, values, base=i * PIECES):
            out[base + piece, :, at] = values.astype(jnp.bfloat16)

        coded_half(h, held, 2 * group + (first + i) % 2, store)


def far_kernel(x_ref, stream_ref, keep, send, held, rows, arrived):
    chip, core, _ = position()
    far = chip_at(chip, FAR)

    def fetch(ref, group, half, target, slot):
        source = ref.at[
            pl.ds(pl.multiple_of(group * GROUP, GROUP), GROUP), half * HALF : (half + 1) * HALF
        ]
        return pltpu.make_async_copy(source, target, arrived.at[slot])

    copies = []
    for i in (4, 3, 5, 2, 6, 1, 7, 0):
        group = chip_at(chip, i)
        for half in range(2):
            copies.append(fetch(x_ref, group, half, held.at[2 * group + half], len(copies)))
    for half in range(2):
        copies.append(fetch(stream_ref, chip, half, rows.at[half], len(copies)))
    for copy in copies:
        copy.start()
    h = hadamard()
    for copy in copies[:2]:
        copy.wait()
    code_group(h, held, far, keep, core, 1)
    code_group(h, held, far, send, 1 - core, 1)
    for copy in copies[2:]:
        copy.wait()


def code_far(local, stream):
    part = jax.ShapeDtypeStruct((PIECES, GROUP, COLS), jnp.bfloat16)
    whole = jax.ShapeDtypeStruct((2 * CHIPS, GROUP, HALF), jnp.bfloat16)
    rows = jax.ShapeDtypeStruct((2, GROUP, HALF), jnp.bfloat16)
    return pl.pallas_call(
        far_kernel,
        out_shape=(part, part, whole, rows),
        in_specs=[pl.BlockSpec(memory_space=pltpu.HBM)] * 2,
        out_specs=(VMEM,) * 4,
        scratch_shapes=[pltpu.SemaphoreType.DMA((2 * CHIPS + 2,))],
        compiler_params=GRANT,
        cost_estimate=SMALL,
    )(local, stream)


def code_kernel(k, held, keep, send):
    chip, core, way = position()
    h = hadamard()
    code_group(h, held, chip_at(chip, way * k), keep, core, 2)
    code_group(h, held, chip_at(chip, -way * k), send, 1 - core, 2)


def code_rows(held, k, after):
    part = jax.ShapeDtypeStruct((2 * PIECES, GROUP, COLS), jnp.bfloat16)
    return pl.pallas_call(
        lambda held_ref, _, *refs: code_kernel(k, held_ref, *refs),
        out_shape=(part, part),
        in_specs=[VMEM, ANY],
        out_specs=(VMEM, VMEM),
        compiler_params=GRANT,
        cost_estimate=SMALL,
    )(held, after)


def own_kernel(held, stream, near_ref, send_ref, rows_ref):
    chip, core, _ = position()
    first = core == 0
    h = hadamard()
    for half in range(2):

        def store(piece, at, values, half=half):
            top, low = values[:OWN], values[OWN:]
            mine = jnp.where(first, top, low).astype(jnp.bfloat16)
            theirs = jnp.where(first, low, top).astype(jnp.bfloat16)
            near_ref[((half + core) % 2) * PIECES + piece, :, at] = mine
            send_ref[((half + 1 - core) % 2) * PIECES + piece, :, at] = theirs

        coded_half(h, held, 2 * chip + half, store)
        for i in range(PIECES):
            rows = stream[half, :, i * COLS : (i + 1) * COLS].astype(jnp.float32)
            rows = jnp.where(first, rows[:OWN], rows[OWN:])
            rows_ref[((half + core) % 2) * PIECES + i] = rows.astype(jnp.bfloat16)


def own_rows(held, stream, after):
    part = jax.ShapeDtypeStruct((2 * PIECES, OWN, COLS), jnp.bfloat16)
    return pl.pallas_call(
        lambda held_ref, stream_ref, _, *refs: own_kernel(held_ref, stream_ref, *refs),
        out_shape=(part, part, part),
        in_specs=[VMEM, VMEM, ANY],
        out_specs=(VMEM,) * 3,
        compiler_params=GRANT,
        cost_estimate=SMALL,
    )(held, stream, after)


def add_kernel(i, keep, got, *rest):
    total = keep[i].astype(jnp.float32) + got[i].astype(jnp.float32)
    for arrived in rest[:-1]:
        total = total + arrived[...].astype(jnp.float32)
    rest[-1][...] = total.astype(jnp.bfloat16)


def add(i, keep, got, arrived):
    blocks = [keep, got] + ([] if arrived is None else [arrived])
    return pl.pallas_call(
        lambda *refs: add_kernel(i, *refs),
        out_shape=jax.ShapeDtypeStruct((GROUP, COLS), jnp.bfloat16),
        in_specs=[VMEM] * len(blocks),
        out_specs=VMEM,
        compiler_params=GRANT,
        cost_estimate=SMALL,
    )(*blocks)


def last_add_kernel(half, keep, got, arrived, same, cross):
    first = position()[1] == 0
    for j in range(PIECES):
        i = half * PIECES + j
        total = keep[i].astype(jnp.float32) + got[i].astype(jnp.float32)
        total = total + arrived[j][...].astype(jnp.float32)
        top, low = total[:OWN], total[OWN:]
        same[j] = jnp.where(first, top, low).astype(jnp.bfloat16)
        cross[j] = jnp.where(first, low, top).astype(jnp.bfloat16)


def last_add(half, keep, got, arrived):
    part = jax.ShapeDtypeStruct((PIECES, OWN, COLS), jnp.bfloat16)
    return pl.pallas_call(
        lambda *refs: last_add_kernel(
            half, refs[0], refs[1], refs[2:-2], *refs[-2:]
        ),
        out_shape=(part, part),
        in_specs=[VMEM] * (PIECES + 2),
        out_specs=(VMEM, VMEM),
        compiler_params=GRANT,
        cost_estimate=SMALL,
    )(keep, got, *arrived)


def norm_kernel(near, rows, got, same0, same1, cross0, cross1, hidden_ref, whole, out0, out1):
    sames, crosses = (same0, same1), (cross1, cross0)
    f32 = jnp.float32
    squares = jnp.zeros((OWN, COLS), f32)
    for half in range(2):
        for j in range(PIECES):
            i = half * PIECES + j
            total = near[i].astype(f32) + got[i].astype(f32)
            total = total + sames[half][j].astype(f32) + crosses[half][j].astype(f32)
            hidden = rows[i].astype(f32) + total * np.float32(BLOCK**-0.5)
            hidden = hidden.astype(jnp.bfloat16)
            hidden_ref[i] = hidden
            hidden = hidden.astype(f32)
            squares = squares + hidden * hidden
    mean = jnp.sum(squares, axis=1, keepdims=True) / D
    inv_rms = lax.rsqrt(mean + np.float32(1e-05))
    for half, out in enumerate((out0, out1)):
        for j in range(PIECES):
            hidden = hidden_ref[half * PIECES + j].astype(f32)
            normed = (hidden * inv_rms).astype(jnp.bfloat16)
            out[j] = normed
            whole[half * PIECES + j] = normed


def norm(*blocks):
    part = jax.ShapeDtypeStruct((PIECES, OWN, COLS), jnp.bfloat16)
    return pl.pallas_call(
        norm_kernel,
        out_shape=(jax.ShapeDtypeStruct((2 * PIECES, OWN, COLS), jnp.bfloat16),) * 2 + (part, part),
        in_specs=[VMEM] * len(blocks),
        out_specs=(VMEM,) * 4,
        compiler_params=GRANT,
        cost_estimate=SMALL,
    )(*blocks)


def split_kernel(block, low, high):
    low[...] = block[:PIECES]
    high[...] = block[PIECES:]


def split(block):
    part = jax.ShapeDtypeStruct((PIECES, OWN, COLS), jnp.bfloat16)
    return pl.pallas_call(
        split_kernel,
        out_shape=(part, part),
        in_specs=[VMEM],
        out_specs=(VMEM, VMEM),
        compiler_params=GRANT,
        cost_estimate=SMALL,
    )(block)


def join_kernel(count, *refs):
    at = 0
    for ref in refs[:count]:
        n = ref.shape[0]
        refs[-1][at : at + n] = ref[...]
        at += n


def join(blocks, after):
    n = sum(b.shape[0] for b in blocks)
    return pl.pallas_call(
        lambda *refs: join_kernel(len(blocks), *refs),
        out_shape=jax.ShapeDtypeStruct((n, OWN, COLS), jnp.bfloat16),
        in_specs=[VMEM] * len(blocks) + [ANY] * len(after),
        out_specs=VMEM,
        compiler_params=GRANT,
        cost_estimate=SMALL,
    )(*blocks, *after)


def put_kernel(places, aliased, *refs):
    sems, out, done = refs[-1], refs[-2], refs[-3]
    blocks = refs[aliased : aliased + len(places)]
    incoming = refs[-4]
    done[...] = jnp.zeros_like(done)
    chip, core, way = position()
    copies = []
    for block, held in zip(blocks, places):
        for i, (offset, rows, half) in enumerate(held):
            for j in range(PIECES):
                cols = pl.ds(pl.multiple_of(((core + half) % 2) * HALF + j * COLS, COLS), COLS)
                if offset is None:
                    target = incoming.at[0, :, cols]
                else:
                    owner = 2 * chip_at(chip, way * offset) + (core + rows) % 2
                    target = out.at[owner, :, cols]
                copies.append(
                    pltpu.make_async_copy(block.at[i * PIECES + j], target, sems.at[len(copies)])
                )
    for copy in copies:
        copy.start()
    for copy in copies:
        copy.wait()


def put(out, blocks, places, after):
    copies = PIECES * sum(len(p) for p in places)
    held = [] if out is None else [pltpu.with_memory_space_constraint(out, pltpu.HBM)]
    whole = pltpu.HBM((2 * CHIPS, OWN, D), jnp.bfloat16)
    rows = pltpu.HBM((1, OWN, D), jnp.bfloat16)
    done = jax.ShapeDtypeStruct((8, BLOCK), jnp.float32)
    with_rows = any(p[0] is None for held_places in places for p in held_places)
    outs = [rows, done, whole] if with_rows else [done, whole]
    space = pl.BlockSpec(memory_space=pltpu.HBM)
    return pl.pallas_call(
        lambda *refs: put_kernel(places, len(held) + len(after), *refs),
        out_shape=outs,
        in_specs=[space] * len(held) + [ANY] * len(after) + [VMEM] * len(blocks),
        out_specs=[space] * (len(outs) - 2) + [VMEM, space],
        scratch_shapes=[pltpu.SemaphoreType.DMA((copies,))],
        input_output_aliases={0: len(outs) - 1} if held else {},
        compiler_params=GRANT,
        cost_estimate=SMALL,
    )(*held, *after, *blocks)


def shards(partials, residual):
    local = pltpu.with_memory_space_constraint(partials[0, 0], pltpu.HBM)
    stream = pltpu.with_memory_space_constraint(residual[0], pltpu.HBM)
    n = 2 * CHIPS

    def onward(block, cross=False):
        route = [(i, (i + 2 - 4 * (i % 2)) % n) for i in range(n)]
        return lax.ppermute(block, "tp", [(i, j ^ 1) if cross else (i, j) for i, j in route])

    def other_core(block):
        return lax.ppermute(block, "tp", [(i, i ^ 1) for i in range(n)])

    moving = [None] * (2 * PIECES)
    keep, send, held, rows = code_far(local, stream)
    for k in range(FAR, 1, -1):
        got = other_core(send)
        order = [i for i in (0, 1, 2, 3) if i < keep.shape[0]]
        sums = {i: add(i, keep, got, moving[i]) for i in order}
        keep, send = code_rows(held, k - 1, send)
        for i in order:
            moving[i] = onward(sums[i])
    got = other_core(send)
    near, send, rows = own_rows(held, rows, send)
    same, cross = [], []
    for half in (0, 1):
        span = slice(half * PIECES, (half + 1) * PIECES)
        mine, theirs = last_add(half, keep, got, moving[span])
        same.append(onward(mine))
        cross.append(onward(theirs, True))
    hidden, whole, *normed = norm(near, rows, other_core(send), *same, *cross)

    sections = lax.axis_size("section")
    theirs = list(split(other_core(whole)))[::-1]

    moving = normed + theirs
    blocks = list(moving)
    places = [[(0, rows, half)] for rows in (0, 1) for half in (0, 1)]
    joined, joined_places = [], []
    for k in range(1, FAR + 1):
        kept = [(rows, half) for rows, half in [(0, 0), (0, 1), (1, 0), (1, 1)] if half == 0 or k < FAR]
        ready = [moving[2 * rows + half] for rows, half in kept]
        if k == FAR:
            ready[-1] = join(ready[-1:], [incoming])
        for (rows, half), block in zip(kept, ready):
            moving[2 * rows + half] = onward(block)
        arrived = [moving[2 * rows + half] for rows, half in kept]
        if k == 1:
            hidden = join([hidden], arrived[2:3])
            incoming = lax.ppermute(
                hidden, "section", [(i, (i + 1) % sections) for i in range(sections)]
            )
        if k == FAR:
            swapped = other_core(join(joined[:8], []))
            swapped_places, joined, joined_places = joined_places[:8], joined[8:], joined_places[8:]
            early = put(None, blocks, places, arrived[:1])
            blocks, places = late, late_places
        joined += arrived
        joined_places += [(k, 1 - rows, 1 - half) for rows, half in kept]
        if k < FAR - 1:
            blocks += arrived
            places += [[(-k, rows, half)] for rows, half in kept]
            if k == 1:
                blocks.append(incoming)
                places.append([(None, 0, 0), (None, 0, 1)])
            late, late_places = [], []
        else:
            late += arrived
            late_places += [[(-k, rows, half)] for rows, half in kept]
    incoming, token, out = early
    last = other_core(join(joined, [token]))
    _, out = put(out, blocks + [swapped], places + [swapped_places], [])
    _, out = put(out, [last], [joined_places], [])
    return (out.reshape(1, 2 * CHIPS * OWN, D), incoming)


def solution(mesh):
    placed = (P("section", "tp", None, None), P("section", None, None))
    return jax.shard_map(
        shards,
        mesh=mesh,
        in_specs=placed,
        out_specs=(P("section", None, None), P("section", "tp", None)),
        check_vma=False,
    )
```
